32 devices in a mesh: uly: 2 (over y), blk: 16 (over z, x, core).
Axes of the slice: x: 2, y: 2, z: 4, core: 2. Of those that a mesh axis runs over, the one named last changes fastest.
Arguments:
- query_proj: bfloat16 [48, 384, 3072], P('blk', 'uly'), may hold values from -16 to 16
- key_proj: bfloat16 [48, 384, 3072], P('blk', 'uly'), may hold values from -16 to 16
- value_proj: bfloat16 [48, 384, 3072], P('blk', 'uly'), may hold values from -6 to 6
- query_gain: float32 [128], replicated, may hold values from 0.5 to 8
- key_gain: float32 [128], replicated, may hold values from 0.5 to 8
- neighbours: int32 [48, 9], P('blk'), may hold values from 0 to 47, as said below
- tile_counts: int32 [48], P('blk'), may hold values from 1 to 9, as said below
Outputs:
- attention: bfloat16 [48, 384, 3072], P('blk', 'uly')
The draws below stay inside these ranges and needn't reach their ends.
Inputs may be any that keep to these rules, and one draw needn't show every extreme that they name: `neighbours`: the first tile_counts[t] entries of row t are distinct tiles; entry 0 is t itself; every entry lies in the slab of tile t or in one of the two slabs beside it, a slab being the tiles with equal index // 3; entries at positions tile_counts[t] and beyond equal t. `tile_counts`: some tile lists 9 tiles.
All inputs are finite; a program needn't handle non-finite values.
Results may differ from the reference program's by a relative error of at most 0.005.
The reference program's roundings to bfloat16 on the way (of `query_norm`, `key_norm` and `rounded`) count: a program that leaves them out, or rounds other values in their place, can miss the bound.
Values may be sent and summed in bfloat16 or wider, within the bound.
A program may use at most 192 MiB of HBM per device.

```python
import jax
import jax.numpy as jnp
from jax import lax

HEADS = 24
HD = 128
TILE = 384
NBMAX = 9
TILES_DEV = 3
TILES = 48


def draw_gain(key):
    spread = jax.random.uniform(key, (HD,))
    gains = 0.5 + spread
    return gains.astype(jnp.float32)


def draw_query_gain(key, part):
    return draw_gain(jax.random.fold_in(key, 21))


def draw_key_gain(key, part):
    return draw_gain(jax.random.fold_in(key, 22))


def draw_query_proj(key, part):
    noise = jax.random.normal(jax.random.fold_in(key, 1), (TILES, TILE, HEADS * HD))
    return jnp.clip(noise, -16.0, 16.0).astype(jnp.bfloat16)


def draw_key_proj(key, part):
    noise = jax.random.normal(jax.random.fold_in(key, 2), (TILES, TILE, HEADS * HD))
    return jnp.clip(noise, -16.0, 16.0).astype(jnp.bfloat16)


def count_table(key):
    slab_count = TILES // TILES_DEV
    tile_idx = jnp.arange(TILES, dtype=jnp.int32)
    slab = tile_idx // TILES_DEV
    lowest = jax.random.randint(jax.random.fold_in(key, 1), (slab_count,), max(NBMAX - 5, 1), NBMAX + 1)
    counts = jax.random.randint(jax.random.fold_in(key, 2), (TILES,), lowest[slab], NBMAX + 1)
    edge = (slab == 0) | (slab == slab_count - 1)
    counts = jnp.where(edge, jnp.minimum(counts, 2 * TILES_DEV), counts)
    chosen = jax.random.randint(jax.random.fold_in(key, 3), (), TILES_DEV, TILES - TILES_DEV)
    return jnp.where(tile_idx == chosen, NBMAX, counts).astype(jnp.int32)


def draw_tile_counts(key, part):
    return count_table(jax.random.fold_in(key, 11))


def draw_neighbours(key, part):
    counts = count_table(jax.random.fold_in(key, 11))
    span = 3 * TILES_DEV
    tile_idx = jnp.arange(TILES, dtype=jnp.int32)
    slab = tile_idx // TILES_DEV
    candidates = (slab[:, None] - 1) * TILES_DEV + jnp.arange(span, dtype=jnp.int32)[None, :]
    usable = (candidates >= 0) & (candidates < TILES) & (candidates != tile_idx[:, None])
    row_keys = jax.random.split(jax.random.fold_in(key, 12), TILES)
    priority = jax.vmap(lambda row_key: jax.random.permutation(row_key, span))(row_keys).astype(jnp.int32)
    sort_keys = jnp.where(usable, priority, priority + span)
    order = jnp.argsort(sort_keys, axis=1)
    picked = jnp.take_along_axis(candidates, order, axis=1)[:, :NBMAX - 1]
    listed = jnp.concatenate([tile_idx[:, None], picked], axis=1)
    position = jnp.arange(NBMAX, dtype=jnp.int32)[None, :]
    return jnp.where(position < counts[:, None], listed, tile_idx[:, None]).astype(jnp.int32)


def block_levels(stream_key, dims, pieces, least, top_value):
    factor_of = 1.0
    for dim, parts in pieces:
        steps = jax.random.uniform(jax.random.fold_in(jax.random.fold_in(stream_key, 6), dim), (parts,), jnp.float32, least / len(pieces), top_value / len(pieces))
        factor_of = factor_of * jnp.repeat(jnp.exp(steps), dims[dim] // parts).reshape((-1,) + (1,) * (len(dims) - 1 - dim))
    return factor_of


def normal_values(key, shape, scale, reach, cuts=(), kind=jnp.bfloat16):
    loudness = block_levels(key, shape, cuts, -0.22, 0.18) if cuts else 1.0
    result = jax.random.normal(key, shape, jnp.float32) * scale * loudness
    return jnp.minimum(jnp.maximum(result, -reach), reach).astype(kind)


def setup_inputs(seed: int = 0) -> dict:
    seeds = jax.random.split(jax.random.key(seed), 8)
    query_proj = draw_query_proj(jax.random.fold_in(seeds[7], 71), 0)
    key_proj = draw_key_proj(jax.random.fold_in(seeds[7], 71), 0)
    value_proj = normal_values(seeds[2], (TILES, TILE, HEADS * HD), 1.0, 6.0, ((0, 16), (1, 2)))
    query_gain = draw_query_gain(jax.random.fold_in(seeds[7], 71), 0)
    key_gain = draw_key_gain(jax.random.fold_in(seeds[7], 71), 0)
    neighbours = draw_neighbours(jax.random.fold_in(seeds[7], 71), 0)
    tile_counts = draw_tile_counts(jax.random.fold_in(seeds[7], 71), 0)
    return {"query_proj": query_proj, "key_proj": key_proj, "value_proj": value_proj, "query_gain": query_gain, "key_gain": key_gain, "neighbours": neighbours, "tile_counts": tile_counts}


def normalize_heads(values_in, gain_vec):
    widened = values_in.astype(jnp.float32)
    widened = widened.reshape(widened.shape[:-1] + (widened.shape[-1] // HD, HD))
    scaled = widened * lax.rsqrt(lax.optimization_barrier(jnp.mean(widened * widened, axis=-1, keepdims=True)) + 1e-06) * gain_vec
    return scaled.astype(jnp.bfloat16).reshape(values_in.shape)

def attend_tile(query_tile, key_tiles, value_tiles, live_count):
    head_count = query_tile.shape[-1] // HD
    rows = query_tile.shape[0]
    inv_root = HD ** (-0.5)
    query_rows = query_tile.reshape(rows, head_count, HD).astype(jnp.float32)
    key_rows = key_tiles.reshape(-1, head_count, HD).astype(jnp.float32)
    value_rows = value_tiles.reshape(-1, head_count, HD).astype(jnp.float32)
    scores = jnp.einsum('qhd,khd->hqk', query_rows, key_rows) * inv_root
    live_keys = jnp.repeat(jnp.arange(key_tiles.shape[0], dtype=jnp.int32) < live_count, key_tiles.shape[1])
    scores = jnp.where(live_keys, scores, jnp.float32(-1e+30))
    row_max = lax.optimization_barrier(jnp.max(scores, axis=-1, keepdims=True))
    weights = jnp.where(live_keys, jnp.exp(scores - row_max), jnp.float32(0.0))
    totals = lax.optimization_barrier(jnp.sum(weights, axis=-1))
    rounded = weights.astype(jnp.bfloat16)
    numerator = jnp.einsum('hqk,khd->qhd', rounded.astype(jnp.float32), value_rows)
    attended = numerator / jnp.transpose(totals)[:, :, None]
    return attended.astype(jnp.bfloat16).reshape(rows, head_count * HD)

def reference(query_proj, key_proj, value_proj, query_gain, key_gain, neighbours, tile_counts):
    query_norm = normalize_heads(query_proj, query_gain)
    key_norm = normalize_heads(key_proj, key_gain)

    def attend(tile_idx):
        slots = neighbours[tile_idx]
        return attend_tile(query_norm[tile_idx], key_norm[slots], value_proj[slots], tile_counts[tile_idx])
    return lax.map(attend, jnp.arange(TILES, dtype=jnp.int32))
```

```python
import functools
import math

import jax
import jax.numpy as jnp
from jax import lax
from jax.experimental import pallas as pl
from jax.experimental.pallas import tpu as pltpu
from jax.sharding import PartitionSpec as P

HD = 128
LANES = 128
MESH = pl.DeviceIdType.MESH


def normalize(rows, gain):
    wide = rows.astype(jnp.float32)
    mean = jnp.mean(wide * wide, axis=-1, keepdims=True)
    return (wide * lax.rsqrt(mean + 1e-06) * gain).astype(jnp.bfloat16)


def kernel(
    nu, nb, groups, width,
    neighbours, counts, qgain, kgain, q, k, v,
    out,
    kv, qbuf, obuf, kn, vs, s0, s1,
    y_send, y_recv, x_send, x_recv, o_send, o_recv, local_sem, own_sem,
):
    tiles, rows, _ = q.shape
    tile = rows * nu
    heads = width // HD
    span = 3 * tiles
    u, b = lax.axis_index("uly"), lax.axis_index("blk")
    first_tile = (b - 1) * tiles
    has_prev, has_next = b > 0, b < nb - 1

    def peer(p):
        return lax.rem(u + p, nu)

    def source(p):
        return lax.rem(u + nu - p, nu)

    def cols(owner, g):
        return pl.ds(pl.multiple_of((owner * groups + g) * width, LANES), width)

    def part(owner):
        return pl.ds(pl.multiple_of(owner * rows, 16), rows)

    barrier = pltpu.get_barrier_semaphore()
    for p in range(1, nu):
        pl.semaphore_signal(barrier, inc=1, device_id=(peer(p), b), device_id_type=MESH)

    @pl.when(has_prev)
    def _():
        pl.semaphore_signal(barrier, inc=1, device_id=(u, b - 1), device_id_type=MESH)

    @pl.when(has_next)
    def _():
        pl.semaphore_signal(barrier, inc=1, device_id=(u, b + 1), device_id_type=MESH)

    pl.semaphore_wait(
        barrier, nu - 1 + has_prev.astype(jnp.int32) + has_next.astype(jnp.int32)
    )

    def y_copy(g, p, kind, arriving):
        target = peer(p)
        owner = source(p) if arriving else u
        src = (k, v, q)[kind].at[:, :, cols(target, g)]
        if kind == 2:
            dst = qbuf.at[g, :, part(owner), :]
        else:
            dst = kv.at[g, kind, pl.ds(tiles, tiles), part(owner), :]
        return pltpu.make_async_remote_copy(
            src_ref=src, dst_ref=dst,
            send_sem=y_send.at[g, p - 1, kind], recv_sem=y_recv.at[g, p - 1, kind],
            device_id=(target, b), device_id_type=MESH,
        )

    def own_copy(g, kind):
        src = (k, v, q)[kind].at[:, :, cols(u, g)]
        if kind == 2:
            dst = qbuf.at[g, :, part(u), :]
        else:
            dst = kv.at[g, kind, pl.ds(tiles, tiles), part(u), :]
        return pltpu.make_async_copy(src, dst, local_sem.at[g, kind])

    def x_copy(g, way, p, kind):
        owner = source(p)
        if p == 0:
            src = (k, v)[kind].at[:, :, cols(u, g)]
        else:
            src = kv.at[g, kind, pl.ds(tiles, tiles), part(owner), :]
        dst = kv.at[g, kind, pl.ds(2 * tiles * way, tiles), part(owner), :]
        return pltpu.make_async_remote_copy(
            src_ref=src, dst_ref=dst,
            send_sem=x_send.at[g, way, p, kind], recv_sem=x_recv.at[g, way, p, kind],
            device_id=(u, b + 1 - 2 * way), device_id_type=MESH,
        )

    def o_copy(g, p, arriving):
        target = peer(p)
        owner = source(p) if arriving else u
        return pltpu.make_async_remote_copy(
            src_ref=obuf.at[g, :, part(target), :],
            dst_ref=out.at[:, :, cols(owner, g)],
            send_sem=o_send.at[g, p - 1], recv_sem=o_recv.at[g, p - 1],
            device_id=(target, b), device_id_type=MESH,
        )

    def own_out(g):
        return pltpu.make_async_copy(
            obuf.at[g, :, part(u), :], out.at[:, :, cols(u, g)], own_sem.at[g]
        )

    def start_x(g, p):
        @pl.when(has_next)
        def _():
            for kind in range(2):
                x_copy(g, 0, p, kind).start()

        @pl.when(has_prev)
        def _():
            for kind in range(2):
                x_copy(g, 1, p, kind).start()

    def start_group(g):
        for kind in range(3):
            for p in range(1, nu):
                y_copy(g, p, kind, False).start()
        start_x(g, 0)
        for kind in range(3):
            own_copy(g, kind).start()

    def forward(g):
        for p in range(1, nu):
            for kind in range(2):
                y_copy(g, p, kind, True).wait_recv()
            start_x(g, p)

    def arrive(g):
        for kind in range(3):
            own_copy(g, kind).wait()
        for p in range(1, nu):
            y_copy(g, p, 2, True).wait_recv()

        @pl.when(has_prev)
        def _():
            for p in range(nu):
                for kind in range(2):
                    x_copy(g, 0, p, kind).wait_recv()

        @pl.when(has_next)
        def _():
            for p in range(nu):
                for kind in range(2):
                    x_copy(g, 1, p, kind).wait_recv()

    unit = math.log2(math.e) * HD ** (-0.5)
    block = tile // 2
    strips = tile // LANES

    def attend(g):
        key_gain = kgain[...]
        query_gain = qgain[...]

        def stage(w, carry):
            for h in range(heads):
                at = slice(h * HD, (h + 1) * HD)
                kn[h, w] = normalize(kv[g, 0, w, :, at], key_gain)
                vs[h, w] = kv[g, 1, w, :, at]
            return carry

        lax.fori_loop(0, span, stage, 0)

        def query_tile(t, carry):
            count = counts[t]
            ids = [jnp.clip(neighbours[t, j] - first_tile, 0, span - 1) for j in range(neighbours.shape[1])]
            live = [j < count for j in range(len(ids))]
            items = [(h, r) for h in range(heads) for r in range(2)]
            refs = (s0, s1)
            query = top = None
            previous = None
            for n in range(len(items) + 1):
                if n < len(items):
                    h, r = items[n]
                    query = normalize(
                        qbuf[g, t, r * block : (r + 1) * block, h * HD : (h + 1) * HD], query_gain
                    )
                    peak = jnp.full((block, LANES), -1e30, jnp.float32)
                if previous is not None:
                    ph, pr, shift = previous
                    total = jnp.zeros((block, LANES), jnp.float32)
                    gathered = jnp.zeros((block, HD), jnp.float32)
                for j in range(len(ids)):
                    if n < len(items):
                        score = lax.dot_general(
                            query, kn[h, ids[j]], (((1,), (1,)), ((), ())),
                            preferred_element_type=jnp.float32,
                        )
                        refs[n % 2][j] = score
                        high = score[:, :LANES]
                        for c in range(1, strips):
                            high = jnp.maximum(high, score[:, c * LANES : (c + 1) * LANES])
                        peak = jnp.maximum(peak, jnp.where(live[j], high, -1e30))
                    if previous is not None:
                        here = jnp.where(live[j], shift, 1e30)
                        weight = jnp.exp2(refs[(n - 1) % 2][j] * unit - here)
                        for c in range(strips):
                            total = total + weight[:, c * LANES : (c + 1) * LANES]
                        gathered = gathered + jnp.dot(
                            weight.astype(jnp.bfloat16), vs[ph, ids[j]],
                            preferred_element_type=jnp.float32,
                        )
                if previous is not None:
                    whole = jnp.sum(total, axis=-1, keepdims=True)
                    obuf[g, t, pr * block : (pr + 1) * block, ph * HD : (ph + 1) * HD] = (
                        gathered / whole
                    ).astype(jnp.bfloat16)
                if n < len(items):
                    previous = (h, r, jnp.max(peak, axis=-1, keepdims=True) * unit)
            return carry

        lax.fori_loop(0, tiles, query_tile, 0)

    start_group(0)
    if groups > 1:
        start_group(1)
    forward(0)

    def step(g, carry):
        @pl.when(g + 2 < groups)
        def _():
            start_group(g + 2)

        @pl.when(g + 1 < groups)
        def _():
            forward(g + 1)

        arrive(g)
        attend(g)
        for p in range(1, nu):
            o_copy(g, p, False).start()
        own_out(g).start()
        return carry

    lax.fori_loop(0, groups, step, 0)

    def drain(g, carry):
        for p in range(1, nu):
            for kind in range(3):
                y_copy(g, p, kind, False).wait_send()
            o_copy(g, p, False).wait_send()
            o_copy(g, p, True).wait_recv()
        own_out(g).wait()

        @pl.when(has_next)
        def _():
            for p in range(nu):
                for kind in range(2):
                    x_copy(g, 0, p, kind).wait_send()

        @pl.when(has_prev)
        def _():
            for p in range(nu):
                for kind in range(2):
                    x_copy(g, 1, p, kind).wait_send()

        return carry

    lax.fori_loop(0, groups, drain, 0)


def body(nu, nb, query_proj, key_proj, value_proj, query_gain, key_gain, neighbours, tile_counts):
    tiles, rows, full = query_proj.shape
    tile = rows * nu
    local_heads = full // HD // nu
    heads = 2 if local_heads % 2 == 0 else 1
    groups = local_heads // heads
    width = heads * HD
    span = 3 * tiles
    listed = neighbours.shape[1]
    any_space = pl.BlockSpec(memory_space=pl.ANY)
    smem = pl.BlockSpec(memory_space=pltpu.SMEM)
    vmem = pl.BlockSpec(memory_space=pltpu.VMEM)
    dma = pltpu.SemaphoreType.DMA
    return pl.pallas_call(
        functools.partial(kernel, nu, nb, groups, width),
        out_shape=jax.ShapeDtypeStruct(query_proj.shape, query_proj.dtype),
        in_specs=[smem, smem, vmem, vmem, any_space, any_space, any_space],
        out_specs=any_space,
        scratch_shapes=[
            pltpu.VMEM((groups, 2, span, tile, width), jnp.bfloat16),
            pltpu.VMEM((groups, tiles, tile, width), jnp.bfloat16),
            pltpu.VMEM((groups, tiles, tile, width), jnp.bfloat16),
            pltpu.VMEM((heads, span, tile, HD), jnp.bfloat16),
            pltpu.VMEM((heads, span, tile, HD), jnp.bfloat16),
            pltpu.VMEM((listed, tile // 2, tile), jnp.float32),
            pltpu.VMEM((listed, tile // 2, tile), jnp.float32),
            dma((groups, max(nu - 1, 1), 3)),
            dma((groups, max(nu - 1, 1), 3)),
            dma((groups, 2, nu, 2)),
            dma((groups, 2, nu, 2)),
            dma((groups, max(nu - 1, 1))),
            dma((groups, max(nu - 1, 1))),
            dma((groups, 3)),
            dma((groups,)),
        ],
        compiler_params=pltpu.CompilerParams(
            collective_id=0, has_side_effects=True, vmem_limit_bytes=56 * 1024 * 1024
        ),
        name="tile_attention",
    )(
        neighbours, tile_counts, query_gain.reshape(1, HD), key_gain.reshape(1, HD),
        query_proj, key_proj, value_proj,
    )


def solution(mesh):
    nu, nb = mesh.shape["uly"], mesh.shape["blk"]
    in_specs = (
        P("blk", "uly", None),
        P("blk", "uly", None),
        P("blk", "uly", None),
        P(),
        P(),
        P("blk", None),
        P("blk"),
    )
    return jax.shard_map(
        functools.partial(body, nu, nb), mesh=mesh, in_specs=in_specs,
        out_specs=P("blk", "uly", None), check_vma=False,
    )
```

```python
import functools
import math

import jax
import jax.numpy as jnp
from jax import lax
from jax.experimental import pallas as pl
from jax.experimental.pallas import tpu as pltpu
from jax.sharding import PartitionSpec as P

HD = 128
LANES = 128
MESH = pl.DeviceIdType.MESH


def normalize(rows, gain):
    wide = rows.astype(jnp.float32)
    mean = jnp.mean(wide * wide, axis=-1, keepdims=True)
    return (wide * lax.rsqrt(mean + 1e-06) * gain).astype(jnp.bfloat16)


def kernel(
    nu, nb, groups, width,
    neighbours, counts, qgain, kgain, q, k, v,
    out,
    kv, qbuf, obuf, kn, vs, s0, s1,
    y_send, y_recv, x_send, x_recv, o_send, o_recv, local_sem, own_sem,
):
    tiles, rows, _ = q.shape
    tile = rows * nu
    span = 3 * tiles
    u, b = lax.axis_index("uly"), lax.axis_index("blk")
    first_tile = (b - 1) * tiles
    has_prev, has_next = b > 0, b < nb - 1

    def peer(p):
        return lax.rem(u + p, nu)

    def source(p):
        return lax.rem(u + nu - p, nu)

    def cols(owner, g):
        return pl.ds(pl.multiple_of((owner * groups + g) * width, LANES), width)

    def part(owner):
        return pl.ds(pl.multiple_of(owner * rows, 16), rows)

    barrier = pltpu.get_barrier_semaphore()
    for p in range(1, nu):
        pl.semaphore_signal(barrier, inc=1, device_id=(peer(p), b), device_id_type=MESH)

    @pl.when(has_prev)
    def _():
        pl.semaphore_signal(barrier, inc=1, device_id=(u, b - 1), device_id_type=MESH)

    @pl.when(has_next)
    def _():
        pl.semaphore_signal(barrier, inc=1, device_id=(u, b + 1), device_id_type=MESH)

    pl.semaphore_wait(
        barrier, nu - 1 + has_prev.astype(jnp.int32) + has_next.astype(jnp.int32)
    )

    def y_copy(g, p, kind, arriving):
        target = peer(p)
        owner = source(p) if arriving else u
        src = (k, v, q)[kind].at[:, :, cols(target, g)]
        if kind == 2:
            dst = qbuf.at[g, :, part(owner), :]
        else:
            dst = kv.at[g, kind, pl.ds(tiles, tiles), part(owner), :]
        return pltpu.make_async_remote_copy(
            src_ref=src, dst_ref=dst,
            send_sem=y_send.at[g, p - 1, kind], recv_sem=y_recv.at[g, p - 1, kind],
            device_id=(target, b), device_id_type=MESH,
        )

    def own_copy(g, kind):
        src = (k, v, q)[kind].at[:, :, cols(u, g)]
        if kind == 2:
            dst = qbuf.at[g, :, part(u), :]
        else:
            dst = kv.at[g, kind, pl.ds(tiles, tiles), part(u), :]
        return pltpu.make_async_copy(src, dst, local_sem.at[g, kind])

    def x_copy(g, way, p, kind):
        owner = source(p)
        if p == 0:
            src = (k, v)[kind].at[:, :, cols(u, g)]
        else:
            src = kv.at[g, kind, pl.ds(tiles, tiles), part(owner), :]
        dst = kv.at[g, kind, pl.ds(2 * tiles * way, tiles), part(owner), :]
        return pltpu.make_async_remote_copy(
            src_ref=src, dst_ref=dst,
            send_sem=x_send.at[g, way, p, kind], recv_sem=x_recv.at[g, way, p, kind],
            device_id=(u, b + 1 - 2 * way), device_id_type=MESH,
        )

    def o_copy(g, p, arriving):
        target = peer(p)
        owner = source(p) if arriving else u
        return pltpu.make_async_remote_copy(
            src_ref=obuf.at[g, :, part(target), :],
            dst_ref=out.at[:, :, cols(owner, g)],
            send_sem=o_send.at[g, p - 1], recv_sem=o_recv.at[g, p - 1],
            device_id=(target, b), device_id_type=MESH,
        )

    def own_out(g):
        return pltpu.make_async_copy(
            obuf.at[g, :, part(u), :], out.at[:, :, cols(u, g)], own_sem.at[g]
        )

    def start_x(g, p):
        @pl.when(has_next)
        def _():
            for kind in range(2):
                x_copy(g, 0, p, kind).start()

        @pl.when(has_prev)
        def _():
            for kind in range(2):
                x_copy(g, 1, p, kind).start()

    def start_group(g):
        for kind in range(3):
            for p in range(1, nu):
                y_copy(g, p, kind, False).start()
        start_x(g, 0)
        for kind in range(3):
            own_copy(g, kind).start()

    def forward(g):
        for p in range(1, nu):
            for kind in range(2):
                y_copy(g, p, kind, True).wait_recv()
            start_x(g, p)

    def arrive(g):
        for kind in range(3):
            own_copy(g, kind).wait()
        for p in range(1, nu):
            y_copy(g, p, 2, True).wait_recv()

        @pl.when(has_prev)
        def _():
            for p in range(nu):
                for kind in range(2):
                    x_copy(g, 0, p, kind).wait_recv()

        @pl.when(has_next)
        def _():
            for p in range(nu):
                for kind in range(2):
                    x_copy(g, 1, p, kind).wait_recv()

    unit = math.log2(math.e) * HD ** (-0.5)
    block = tile // 2
    strips = tile // LANES

    def attend(g, before_rest):
        key_gain = kgain[...]
        query_gain = qgain[...]

        def stage(w, carry):
            kn[w] = normalize(kv[g, 0, w], key_gain)
            vs[w] = kv[g, 1, w]
            return carry

        lax.fori_loop(0, span, stage, 0)

        items = [(t, r) for t in range(tiles) for r in range(2)]
        run_items(g, query_gain, items[:2])
        before_rest()
        run_items(g, query_gain, items[2:])

    def run_items(g, query_gain, items):
        refs = (s0, s1)
        listed = neighbours.shape[1]
        chunks = [tuple(range(j, min(j + 2, listed))) for j in range(0, listed, 2)]
        lists = {}
        for t in sorted({t for t, _ in items}):
            ids = [jnp.clip(neighbours[t, j] - first_tile, 0, span - 1) for j in range(listed)]
            lists[t] = ids, [j < counts[t] for j in range(listed)]
        previous = None
        for n in range(len(items) + 1):
            if n < len(items):
                t, r = items[n]
                ids, live = lists[t]
                query = normalize(qbuf[g, t, r * block : (r + 1) * block, :], query_gain)
                peak = jnp.full((block, LANES), -1e30, jnp.float32)
            if previous is not None:
                pt, pr, shift = previous
                pids, plive = lists[pt]
                total = jnp.zeros((block, LANES), jnp.float32)
                gathered = jnp.zeros((block, HD), jnp.float32)
            for chunk in chunks:
                if n < len(items):
                    keys = jnp.concatenate([kn[ids[j]] for j in chunk], axis=0)
                    score = lax.dot_general(
                        query, keys, (((1,), (1,)), ((), ())), preferred_element_type=jnp.float32
                    )
                    for i, j in enumerate(chunk):
                        mine = score[:, i * tile : (i + 1) * tile]
                        refs[n % 2][j] = mine
                        high = mine[:, :LANES]
                        for c in range(1, strips):
                            high = jnp.maximum(high, mine[:, c * LANES : (c + 1) * LANES])
                        peak = jnp.maximum(peak, jnp.where(live[j], high, -1e30))
                if previous is not None:
                    rounded = []
                    for j in chunk:
                        here = jnp.where(plive[j], shift, 1e30)
                        weight = jnp.exp2(refs[(n - 1) % 2][j] * unit - here)
                        for c in range(strips):
                            total = total + weight[:, c * LANES : (c + 1) * LANES]
                        rounded.append(weight.astype(jnp.bfloat16))
                    gathered = gathered + jnp.dot(
                        jnp.concatenate(rounded, axis=1),
                        jnp.concatenate([vs[pids[j]] for j in chunk], axis=0),
                        preferred_element_type=jnp.float32,
                    )
            if previous is not None:
                whole = jnp.sum(total, axis=-1, keepdims=True)
                obuf[g, pt, pr * block : (pr + 1) * block, :] = (gathered / whole).astype(
                    jnp.bfloat16
                )
            if n < len(items):
                previous = (t, r, jnp.max(peak, axis=-1, keepdims=True) * unit)

    start_group(0)
    if groups > 1:
        start_group(1)
    forward(0)

    def step(g, carry):
        def forward_next():
            @pl.when(g + 1 < groups)
            def _():
                forward(g + 1)

        arrive(g)

        @pl.when(g + 2 < groups)
        def _():
            start_group(g + 2)

        attend(g, forward_next)
        for p in range(1, nu):
            o_copy(g, p, False).start()
        own_out(g).start()
        return carry

    lax.fori_loop(0, groups, step, 0)

    def drain(g, carry):
        for p in range(1, nu):
            for kind in range(3):
                y_copy(g, p, kind, False).wait_send()
            o_copy(g, p, False).wait_send()
            o_copy(g, p, True).wait_recv()
        own_out(g).wait()

        @pl.when(has_next)
        def _():
            for p in range(nu):
                for kind in range(2):
                    x_copy(g, 0, p, kind).wait_send()

        @pl.when(has_prev)
        def _():
            for p in range(nu):
                for kind in range(2):
                    x_copy(g, 1, p, kind).wait_send()

        return carry

    lax.fori_loop(0, groups, drain, 0)


def body(nu, nb, query_proj, key_proj, value_proj, query_gain, key_gain, neighbours, tile_counts):
    tiles, rows, full = query_proj.shape
    tile = rows * nu
    groups = full // HD // nu
    width = HD
    span = 3 * tiles
    listed = neighbours.shape[1]
    any_space = pl.BlockSpec(memory_space=pl.ANY)
    smem = pl.BlockSpec(memory_space=pltpu.SMEM)
    vmem = pl.BlockSpec(memory_space=pltpu.VMEM)
    dma = pltpu.SemaphoreType.DMA
    return pl.pallas_call(
        functools.partial(kernel, nu, nb, groups, width),
        out_shape=jax.ShapeDtypeStruct(query_proj.shape, query_proj.dtype),
        in_specs=[smem, smem, vmem, vmem, any_space, any_space, any_space],
        out_specs=any_space,
        scratch_shapes=[
            pltpu.VMEM((groups, 2, span, tile, width), jnp.bfloat16),
            pltpu.VMEM((groups, tiles, tile, width), jnp.bfloat16),
            pltpu.VMEM((groups, tiles, tile, width), jnp.bfloat16),
            pltpu.VMEM((span, tile, HD), jnp.bfloat16),
            pltpu.VMEM((span, tile, HD), jnp.bfloat16),
            pltpu.VMEM((listed, tile // 2, tile), jnp.float32),
            pltpu.VMEM((listed, tile // 2, tile), jnp.float32),
            dma((groups, max(nu - 1, 1), 3)),
            dma((groups, max(nu - 1, 1), 3)),
            dma((groups, 2, nu, 2)),
            dma((groups, 2, nu, 2)),
            dma((groups, max(nu - 1, 1))),
            dma((groups, max(nu - 1, 1))),
            dma((groups, 3)),
            dma((groups,)),
        ],
        compiler_params=pltpu.CompilerParams(
            collective_id=0, has_side_effects=True, vmem_limit_bytes=56 * 1024 * 1024
        ),
        name="tile_attention",
    )(
        neighbours, tile_counts, query_gain.reshape(1, HD), key_gain.reshape(1, HD),
        query_proj, key_proj, value_proj,
    )


def solution(mesh):
    nu, nb = mesh.shape["uly"], mesh.shape["blk"]
    in_specs = (
        P("blk", "uly", None),
        P("blk", "uly", None),
        P("blk", "uly", None),
        P(),
        P(),
        P("blk", None),
        P("blk"),
    )
    return jax.shard_map(
        functools.partial(body, nu, nb), mesh=mesh, in_specs=in_specs,
        out_specs=P("blk", "uly", None), check_vma=False,
    )
```

```python
import functools
import math

import jax
import jax.numpy as jnp
from jax import lax
from jax.experimental import pallas as pl
from jax.experimental.pallas import tpu as pltpu
from jax.sharding import PartitionSpec as P

HD = 128
LANES = 128
MESH = pl.DeviceIdType.MESH


def normalize(rows, gain):
    wide = rows.astype(jnp.float32)
    mean = jnp.mean(wide * wide, axis=-1, keepdims=True)
    return (wide * lax.rsqrt(mean + 1e-06) * gain).astype(jnp.bfloat16)


def kernel(
    nu, nb, groups, width,
    neighbours, counts, qgain, kgain, q, k, v,
    out,
    kv, qbuf, obuf, kn, vs, s0, s1,
    y_send, y_recv, x_send, x_recv, o_send, o_recv, local_sem, own_sem,
):
    tiles, rows, _ = q.shape
    tile = rows * nu
    span = 3 * tiles
    u, b = lax.axis_index("uly"), lax.axis_index("blk")
    first_tile = (b - 1) * tiles
    has_prev, has_next = b > 0, b < nb - 1

    def peer(p):
        return lax.rem(u + p, nu)

    def source(p):
        return lax.rem(u + nu - p, nu)

    def cols(owner, g):
        return pl.ds(pl.multiple_of((owner * groups + g) * width, LANES), width)

    def part(owner):
        return pl.ds(pl.multiple_of(owner * rows, 16), rows)

    barrier = pltpu.get_barrier_semaphore()
    for p in range(1, nu):
        pl.semaphore_signal(barrier, inc=1, device_id=(peer(p), b), device_id_type=MESH)

    @pl.when(has_prev)
    def _():
        pl.semaphore_signal(barrier, inc=1, device_id=(u, b - 1), device_id_type=MESH)

    @pl.when(has_next)
    def _():
        pl.semaphore_signal(barrier, inc=1, device_id=(u, b + 1), device_id_type=MESH)

    pl.semaphore_wait(
        barrier, nu - 1 + has_prev.astype(jnp.int32) + has_next.astype(jnp.int32)
    )

    def y_copy(g, p, kind, arriving):
        target = peer(p)
        owner = source(p) if arriving else u
        src = (k, v, q)[kind].at[:, :, cols(target, g)]
        if kind == 2:
            dst = qbuf.at[g, :, part(owner), :]
        else:
            dst = kv.at[g, kind, pl.ds(tiles, tiles), part(owner), :]
        return pltpu.make_async_remote_copy(
            src_ref=src, dst_ref=dst,
            send_sem=y_send.at[g, p - 1, kind], recv_sem=y_recv.at[g, p - 1, kind],
            device_id=(target, b), device_id_type=MESH,
        )

    def own_copy(g, kind):
        src = (k, v, q)[kind].at[:, :, cols(u, g)]
        if kind == 2:
            dst = qbuf.at[g, :, part(u), :]
        else:
            dst = kv.at[g, kind, pl.ds(tiles, tiles), part(u), :]
        return pltpu.make_async_copy(src, dst, local_sem.at[g, kind])

    def x_copy(g, way, p, kind):
        owner = source(p)
        if p == 0:
            src = (k, v)[kind].at[:, :, cols(u, g)]
        else:
            src = kv.at[g, kind, pl.ds(tiles, tiles), part(owner), :]
        dst = kv.at[g, kind, pl.ds(2 * tiles * way, tiles), part(owner), :]
        return pltpu.make_async_remote_copy(
            src_ref=src, dst_ref=dst,
            send_sem=x_send.at[g, way, p, kind], recv_sem=x_recv.at[g, way, p, kind],
            device_id=(u, b + 1 - 2 * way), device_id_type=MESH,
        )

    def o_copy(g, p, arriving):
        target = peer(p)
        owner = source(p) if arriving else u
        return pltpu.make_async_remote_copy(
            src_ref=obuf.at[g, :, part(target), :],
            dst_ref=out.at[:, :, cols(owner, g)],
            send_sem=o_send.at[g, p - 1], recv_sem=o_recv.at[g, p - 1],
            device_id=(target, b), device_id_type=MESH,
        )

    def own_out(g):
        return pltpu.make_async_copy(
            obuf.at[g, :, part(u), :], out.at[:, :, cols(u, g)], own_sem.at[g]
        )

    def start_x(g, p):
        @pl.when(has_next)
        def _():
            for kind in range(2):
                x_copy(g, 0, p, kind).start()

        @pl.when(has_prev)
        def _():
            for kind in range(2):
                x_copy(g, 1, p, kind).start()

    def start_y(g):
        for kind in range(3):
            for p in range(1, nu):
                y_copy(g, p, kind, False).start()
        for kind in range(3):
            own_copy(g, kind).start()

    def ahead(act, g):
        @pl.when(g < groups)
        def _():
            act(g)

    def forward(g):
        for p in range(1, nu):
            for kind in range(2):
                y_copy(g, p, kind, True).wait_recv()
            start_x(g, p)

    def arrive_here(g):
        for kind in range(3):
            own_copy(g, kind).wait()
        for p in range(1, nu):
            y_copy(g, p, 2, True).wait_recv()

    def arrive_beside(g, way):
        @pl.when((has_prev, has_next)[way])
        def _():
            for p in range(nu):
                for kind in range(2):
                    x_copy(g, way, p, kind).wait_recv()

    unit = math.log2(math.e) * HD ** (-0.5)
    block = tile // 2
    strips = tile // LANES

    def attend(g, before_first, before_rest):
        key_gain = kgain[...]
        query_gain = qgain[...]

        def stage(w, carry):
            kn[w] = normalize(kv[g, 0, w], key_gain)
            vs[w] = kv[g, 1, w]
            return carry

        arrive_here(g)
        lax.fori_loop(tiles, 2 * tiles, stage, 0)
        for way in range(2):
            arrive_beside(g, way)
            lax.fori_loop(2 * tiles * way, (2 * way + 1) * tiles, stage, 0)
        before_first()

        items = [(t, r) for t in range(tiles) for r in range(2)]
        run_items(g, query_gain, items[:2])
        before_rest()
        run_items(g, query_gain, items[2:])

    def run_items(g, query_gain, items):
        refs = (s0, s1)
        listed = neighbours.shape[1]
        chunks = [tuple(range(j, min(j + 2, listed))) for j in range(0, listed, 2)]
        lists = {}
        for t in sorted({t for t, _ in items}):
            ids = [jnp.clip(neighbours[t, j] - first_tile, 0, span - 1) for j in range(listed)]
            lists[t] = ids, [j < counts[t] for j in range(listed)]
        previous = None
        for n in range(len(items) + 1):
            if n < len(items):
                t, r = items[n]
                ids, live = lists[t]
                query = normalize(qbuf[g, t, r * block : (r + 1) * block, :], query_gain)
                peak = jnp.full((block, LANES), -1e30, jnp.float32)
            if previous is not None:
                pt, pr, shift = previous
                pids, plive = lists[pt]
                total = jnp.zeros((block, LANES), jnp.float32)
                gathered = jnp.zeros((block, HD), jnp.float32)
            for chunk in chunks:
                if n < len(items):
                    keys = jnp.concatenate([kn[ids[j]] for j in chunk], axis=0)
                    score = lax.dot_general(
                        query, keys, (((1,), (1,)), ((), ())), preferred_element_type=jnp.float32
                    )
                    for i, j in enumerate(chunk):
                        mine = score[:, i * tile : (i + 1) * tile]
                        refs[n % 2][j] = mine
                        high = mine[:, :LANES]
                        for c in range(1, strips):
                            high = jnp.maximum(high, mine[:, c * LANES : (c + 1) * LANES])
                        peak = jnp.maximum(peak, jnp.where(live[j], high, -1e30))
                if previous is not None:
                    rounded = []
                    for j in chunk:
                        here = jnp.where(plive[j], shift, 1e30)
                        weight = jnp.exp2(refs[(n - 1) % 2][j] * unit - here)
                        for c in range(strips):
                            total = total + weight[:, c * LANES : (c + 1) * LANES]
                        rounded.append(weight.astype(jnp.bfloat16))
                    gathered = gathered + jnp.dot(
                        jnp.concatenate(rounded, axis=1),
                        jnp.concatenate([vs[pids[j]] for j in chunk], axis=0),
                        preferred_element_type=jnp.float32,
                    )
            if previous is not None:
                whole = jnp.sum(total, axis=-1, keepdims=True)
                obuf[g, pt, pr * block : (pr + 1) * block, :] = (gathered / whole).astype(
                    jnp.bfloat16
                )
            if n < len(items):
                previous = (t, r, jnp.max(peak, axis=-1, keepdims=True) * unit)

    for g in range(min(3, groups)):
        start_y(g)
        start_x(g, 0)
    forward(0)
    if groups > 3:
        start_y(3)

    def step(g, carry):
        def before_first():
            @pl.when(g == 0)
            def _():
                ahead(forward, g + 1)
                ahead(start_y, g + 4)
                ahead(lambda n: start_x(n, 0), g + 3)

            ahead(start_y, g + 5)
            ahead(lambda n: start_x(n, 0), g + 4)

        attend(g, before_first, lambda: ahead(forward, g + 2))
        for p in range(1, nu):
            o_copy(g, p, False).start()
        own_out(g).start()
        return carry

    lax.fori_loop(0, groups, step, 0)

    def drain(g, carry):
        for p in range(1, nu):
            for kind in range(3):
                y_copy(g, p, kind, False).wait_send()
            o_copy(g, p, False).wait_send()
            o_copy(g, p, True).wait_recv()
        own_out(g).wait()

        @pl.when(has_next)
        def _():
            for p in range(nu):
                for kind in range(2):
                    x_copy(g, 0, p, kind).wait_send()

        @pl.when(has_prev)
        def _():
            for p in range(nu):
                for kind in range(2):
                    x_copy(g, 1, p, kind).wait_send()

        return carry

    lax.fori_loop(0, groups, drain, 0)


def body(nu, nb, query_proj, key_proj, value_proj, query_gain, key_gain, neighbours, tile_counts):
    tiles, rows, full = query_proj.shape
    tile = rows * nu
    groups = full // HD // nu
    width = HD
    span = 3 * tiles
    listed = neighbours.shape[1]
    any_space = pl.BlockSpec(memory_space=pl.ANY)
    smem = pl.BlockSpec(memory_space=pltpu.SMEM)
    vmem = pl.BlockSpec(memory_space=pltpu.VMEM)
    dma = pltpu.SemaphoreType.DMA
    return pl.pallas_call(
        functools.partial(kernel, nu, nb, groups, width),
        out_shape=jax.ShapeDtypeStruct(query_proj.shape, query_proj.dtype),
        in_specs=[smem, smem, vmem, vmem, any_space, any_space, any_space],
        out_specs=any_space,
        scratch_shapes=[
            pltpu.VMEM((groups, 2, span, tile, width), jnp.bfloat16),
            pltpu.VMEM((groups, tiles, tile, width), jnp.bfloat16),
            pltpu.VMEM((groups, tiles, tile, width), jnp.bfloat16),
            pltpu.VMEM((span, tile, HD), jnp.bfloat16),
            pltpu.VMEM((span, tile, HD), jnp.bfloat16),
            pltpu.VMEM((listed, tile // 2, tile), jnp.float32),
            pltpu.VMEM((listed, tile // 2, tile), jnp.float32),
            dma((groups, max(nu - 1, 1), 3)),
            dma((groups, max(nu - 1, 1), 3)),
            dma((groups, 2, nu, 2)),
            dma((groups, 2, nu, 2)),
            dma((groups, max(nu - 1, 1))),
            dma((groups, max(nu - 1, 1))),
            dma((groups, 3)),
            dma((groups,)),
        ],
        compiler_params=pltpu.CompilerParams(
            collective_id=0, has_side_effects=True, vmem_limit_bytes=56 * 1024 * 1024
        ),
        name="tile_attention",
    )(
        neighbours, tile_counts, query_gain.reshape(1, HD), key_gain.reshape(1, HD),
        query_proj, key_proj, value_proj,
    )


def solution(mesh):
    nu, nb = mesh.shape["uly"], mesh.shape["blk"]
    in_specs = (
        P("blk", "uly", None),
        P("blk", "uly", None),
        P("blk", "uly", None),
        P(),
        P(),
        P("blk", None),
        P("blk"),
    )
    return jax.shard_map(
        functools.partial(body, nu, nb), mesh=mesh, in_specs=in_specs,
        out_specs=P("blk", "uly", None), check_vma=False,
    )
```
